256 devices in a mesh: row: 8 (over x, core), col: 32 (over y, z).
Axes of the slice: x: 4, y: 4, z: 8, core: 2. Of those that a mesh axis runs over, the one named last changes fastest.
Arguments:
- a_block: float32 [4, 4096, 16384], P(None, 'row', 'col'), may hold values from -6 to 6
- l_panel: float32 [1024, 4, 4096], P('col', None, 'row'), may hold values from -0.1875 to 0.1875
- inverses: float32 [2, 512, 512], replicated, as said below
Outputs:
- reduced: float32 [4, 4096, 16384], P(None, 'row', 'col')
- right_out: float32 [1024, 4, 4096], P('col', None, 'row')
The draws below stay inside these ranges and needn't reach their ends.
Inputs may be any that keep to these rules, and one draw needn't show every extreme that they name: Each inverses[t] is lower triangular with diagonal entries from 1 to 2.5.
All inputs are finite; a program needn't handle non-finite values.
Results may differ from the reference program's by a relative error of at most 0.000071.
Values sent between devices are 32-bit elements; how exact they have to be, the bound alone decides.
No kernel may reach another device: no remote copies, remote signals or barrier semaphores. Data moves between devices by JAX's collectives and lax.ppermute only.
A program may use at most 128 MiB of HBM per device.

```python
import jax
import jax.numpy as jnp
from jax import lax

NB = 512
RCYC = 4
N = 16384
N_ROW = 8


def draw_inverses(key, part):
    key_diag = jax.random.fold_in(key, 11)
    key_off = jax.random.fold_in(key, 12)
    diagonal = jax.random.uniform(key_diag, (2, NB), jnp.float32, 1.0, 2.5)
    off_diag = jax.random.normal(key_off, (2, NB, NB), jnp.float32) * (0.5 / NB ** 0.5)
    row_ids = lax.broadcasted_iota(jnp.int32, (NB, NB), 0)
    col_ids = lax.broadcasted_iota(jnp.int32, (NB, NB), 1)
    below = (row_ids > col_ids).astype(jnp.float32)
    on_diag = (row_ids == col_ids).astype(jnp.float32)
    return off_diag * below[None] + diagonal[:, :, None] * on_diag[None]


def shard_levels(rng, shape, split, least, top_value):
    def one(axis_at, shards_of):
        heights = jax.random.uniform(jax.random.fold_in(jax.random.fold_in(rng, 6), axis_at), (shards_of,), jnp.float32, least / len(split), top_value / len(split))
        return jnp.repeat(jnp.exp(heights), shape[axis_at] // shards_of).reshape((-1,) + (1,) * (len(shape) - axis_at - 1))

    loudness = one(*split[0])
    for cut in split[1:]:
        loudness = loudness * one(*cut)
    return loudness


def gaussian(stream_key, extent, scale, limit, shards=(), dtype=jnp.bfloat16):
    array = scale * jax.random.normal(stream_key, extent, jnp.float32)
    if shards:
        array = array * shard_levels(stream_key, extent, shards, -0.22, 0.18)
    return jnp.clip(array, -limit, limit).astype(dtype)


def setup_inputs(seed: int = 0) -> dict:
    key_of = jax.random.split(jax.random.key(seed), 4)
    return {
        "a_block": gaussian(key_of[0], (RCYC, N_ROW * NB, N), 1.0, 6.0, ((1, 8), (2, 32)), jnp.float32),
        "l_panel": gaussian(key_of[1], (2 * NB, RCYC, N_ROW * NB), (2 * NB) ** -0.5, 0.1875, ((0, 32), (2, 8)), jnp.float32),
        "inverses": draw_inverses(jax.random.fold_in(key_of[3], 71), 0),
    }


def reference(a_block, l_panel, inverses):
    highest = lax.Precision.HIGHEST
    whole_a = a_block.reshape(N, N)
    l_trans = l_panel.reshape(2 * NB, N)
    w_first = jnp.dot(inverses[0], whole_a[0:NB], precision=highest, preferred_element_type=jnp.float32)
    coupling = jnp.dot(l_trans[0:NB, NB:2 * NB].T, w_first, precision=highest, preferred_element_type=jnp.float32)
    w_second = jnp.dot(inverses[1], whole_a[NB:2 * NB] - coupling, precision=highest, preferred_element_type=jnp.float32)
    panels = jnp.concatenate([w_first, w_second], axis=0)
    trailing = whole_a[2 * NB:] - jnp.dot(l_trans[:, 2 * NB:].T, panels, precision=highest, preferred_element_type=jnp.float32)
    reduced = jnp.concatenate([panels, trailing], axis=0).reshape(a_block.shape)
    y_first = jnp.dot(panels[:, 0:NB], inverses[0].T, precision=highest, preferred_element_type=jnp.float32)
    others = panels[:, NB:] - jnp.dot(y_first, l_trans[0:NB, NB:], precision=highest, preferred_element_type=jnp.float32)
    right_out = jnp.concatenate([y_first, others], axis=1).reshape(l_panel.shape)
    return reduced, right_out
```

```python
import jax
import jax.numpy as jnp
from jax import lax
from jax.experimental import pallas as pl
from jax.experimental.pallas import tpu as pltpu
from jax.sharding import PartitionSpec as P

ROWS, Y, Z = 8, 4, 8
COLS = Y * Z
HIGH = lax.Precision.HIGH
Y_ORDER = (0, 1, -1, -2)
Z_ORDER = (0, 1, -1, -2, 2, 3, -3, -4)


def flat(r, y, z):
    return r * COLS + (y % Y) * Z + z % Z


def permute(x, pairs):
    return lax.ppermute(x, ("row", "col"), pairs)


def neighbour_pairs(axis, step):
    pairs = []
    for r in range(ROWS):
        for y in range(Y):
            for z in range(Z):
                at = y if axis == "y" else z
                side = 1 if ((at + r) % 2 == 0) == (step % 2 == 1) else -1
                to = flat(r, y + side, z) if axis == "y" else flat(r, y, z + side)
                pairs.append((flat(r, y, z), to))
    return pairs


def ring_gather(x, axis):
    size = Y if axis == "y" else Z
    got = permute(x, neighbour_pairs(axis, 1))
    blocks = [x, got]
    held = jnp.concatenate(blocks, axis=0)
    for step in range(2, size // 2 + 1):
        held = permute(held, neighbour_pairs(axis, step))
        blocks.append(held)
    return jnp.concatenate(blocks, axis=0)


def to_other_chips(x):
    row = lax.axis_index("row")
    chip = row // 2
    mine = x
    for j in (1, 3, 2):
        got = lax.ppermute(x, "row", [(0, 2 * j), (1, 2 * j + 1)])
        mine = jnp.where(chip == j, got, mine)
    return mine


def swap_cores(x):
    return lax.ppermute(x, "row", [(r, r ^ 1) for r in range(ROWS)])


def reorder_kernel(index_ref, x_ref, o_ref):
    def body(i, carry):
        o_ref[pl.ds(pl.multiple_of(i * 16, 16), 16), :] = x_ref[
            pl.ds(pl.multiple_of(index_ref[i] * 16, 16), 16), :
        ]
        return carry

    lax.fori_loop(0, index_ref.shape[0], body, 0)


def reorder(x, index):
    return pl.pallas_call(
        reorder_kernel,
        out_shape=jax.ShapeDtypeStruct(x.shape, x.dtype),
        grid_spec=pltpu.PrefetchScalarGridSpec(
            num_scalar_prefetch=1,
            grid=(1,),
            in_specs=[pl.BlockSpec(x.shape, lambda i, s: (0, 0))],
            out_specs=pl.BlockSpec(x.shape, lambda i, s: (0, 0)),
        ),
        compiler_params=pltpu.CompilerParams(vmem_limit_bytes=24 * 2**20),
    )(index, x)


def product(left, right_side):
    return jnp.dot(left, right_side, precision=HIGH, preferred_element_type=jnp.float32)


def from_left(left, right_side):
    return lax.dot_general(
        left,
        right_side,
        (((0,), (0,)), ((), ())),
        precision=HIGH,
        preferred_element_type=jnp.float32,
    )


def on_device(a_block, l_panel, inverses):
    row, col = lax.axis_index("row"), lax.axis_index("col")
    core, chip, y, z = row % 2, row // 2, col // Z, col % Z

    piece = l_panel[:, 0, :]
    piece = to_other_chips(piece)
    other = swap_cores(piece)
    piece = jnp.where(core == 1, piece, other)
    swapped = permute(piece, [(flat(r, i, k), flat(r, i ^ 1, k)) for r in range(ROWS) for i in range(Y) for k in range(Z)])
    pair = jnp.stack([jnp.where(y == 0, piece, swapped), jnp.where(y == 0, swapped, piece)])
    sent = permute(pair, [(flat(r, i, k), flat(r, 3 - i, k)) for r in range(ROWS) for i in range(Y) for k in range(Z)])
    pair = jnp.where(y < 2, pair, sent)
    gathered = ring_gather(pair[None], "z")
    z_side = jnp.where((z + core) % 2 == 0, 1, -1)
    y_side = jnp.where((y + core) % 2 == 0, 1, -1)
    z_list = (z + z_side * jnp.array(Z_ORDER, jnp.int32)) % Z
    y_list = (y + y_side * jnp.array(Y_ORDER, jnp.int32)) % Y

    tile = to_other_chips(a_block[0])
    other = swap_cores(tile)
    first_rows = jnp.where(core == 0, tile, other)
    second_rows = jnp.where(core == 0, other, tile)

    shard = l_panel.reshape(32, 2048)
    l_a = ring_gather(ring_gather(shard[:16], "y"), "z")
    l_b = ring_gather(ring_gather(shard[16:], "z"), "y")

    w_first = product(inverses[0], first_rows)
    w_blocks = w_first.reshape(2, Z, 32, 512).transpose(1, 0, 2, 3).reshape(Z * 4, 16, 512)
    z_index = (z_list[:, None] * 4 + jnp.arange(4, dtype=jnp.int32)[None, :]).reshape(-1)
    w_ordered = reorder(w_blocks.reshape(512, 512), z_index)
    coupling = from_left(gathered.reshape(512, 512), w_ordered)
    w_second = product(inverses[1], second_rows - coupling)
    panels = jnp.concatenate([w_first, w_second], axis=0)

    block_of = lambda yy, zz, half: (yy * Z + zz) * 2 + half
    order = jnp.concatenate([
        block_of(y_list[None, :], z_list[:, None], 0).reshape(-1),
        block_of(y_list[:, None], z_list[None, :], 1).reshape(-1),
    ])

    pieces = panels.reshape(COLS, 2, 16, 4, 128)
    pieces = lax.dynamic_index_in_dim(pieces, core, 1, keepdims=False)
    pieces = lax.dynamic_index_in_dim(pieces, chip, 2, keepdims=False)
    pieces = lax.all_to_all(pieces, "col", 0, 0, tiled=True).reshape(Y, Z, 16, 128)
    first_tile = jnp.broadcast_to(pieces[0, 0], (ROWS, 1, 16, 128))
    pieces = jnp.concatenate([pieces.transpose(1, 0, 2, 3), first_tile], axis=1)
    pieces = lax.all_to_all(pieces, "row", 0, 0, tiled=True).reshape(4, 2, Y + 1, 16, 128)
    own = pieces.transpose(2, 1, 3, 0, 4).reshape(Y + 1, 32, 512)

    panels_ordered = reorder(panels, order)
    remaining = a_block.reshape(2048, 512) - from_left(l_a, panels_ordered[:512]) - from_left(l_b, panels_ordered[512:])
    remaining = remaining.reshape(4, 512, 512)
    top = jnp.where(row == 0, w_first, jnp.where(row == 1, w_second, remaining[0]))
    reduced = remaining.at[0].set(top)

    y_first = lax.dot_general(inverses[0], own[Y], (((1,), (1,)), ((), ())), precision=HIGH, preferred_element_type=jnp.float32)
    y_all = jnp.concatenate([y_first, jnp.zeros_like(y_first)], axis=0)
    y_ordered = reorder(y_all, order)
    solved = from_left(y_ordered[:512], l_a) + from_left(y_ordered[512:], l_b)
    right_out = own[:Y].transpose(1, 0, 2) - solved.reshape(32, 4, 512)
    right_out = right_out.at[:, 0, :].set(jnp.where(row == 0, y_first.T, right_out[:, 0, :]))
    return (reduced, right_out)


def solution(mesh):
    return jax.shard_map(
        on_device,
        mesh=mesh,
        in_specs=(P(None, "row", "col"), P("col", None, "row"), P()),
        out_specs=(P(None, "row", "col"), P("col", None, "row")),
        check_vma=False,
    )
```

```python
import jax
import jax.numpy as jnp
from jax import lax
from jax.experimental import pallas as pl
from jax.experimental.pallas import tpu as pltpu
from jax.sharding import PartitionSpec as P

ROWS, Y, Z = 8, 4, 8
COLS = Y * Z


def flat(r, y, z):
    return r * COLS + (y % Y) * Z + z % Z


def permute(x, pairs):
    return lax.ppermute(x, ("row", "col"), pairs)


def tick(*values):
    return lax.optimization_barrier(values)


def along_x(x, j, cores):
    return lax.ppermute(x, "row", [(c, 2 * j + c) for c in cores])


def along_y(x, rows, to):
    return permute(x, [(flat(r, i, k), flat(r, to[i], k)) for r in rows for i in (0, 1) for k in range(Z)])


def swap_cores(x):
    return lax.ppermute(x, "row", [(r, r ^ 1) for r in range(ROWS)])


def from_z(x, distance):
    return permute(x, [
        (flat(r, i, k + (distance if r % 2 else -distance)), flat(r, i, k))
        for r in range(ROWS) for i in range(Y) for k in range(Z)
    ])


def along_ring_x(x, step):
    return lax.ppermute(x, "row", [(r, (r + 2 * step) % ROWS) for r in range(ROWS)])


def halves(x):
    high = x.astype(jnp.bfloat16)
    return high, (x - high.astype(jnp.float32)).astype(jnp.bfloat16)


def dot3(left, right_side, dims):
    dot = lambda u, v: lax.dot_general(u, v, (dims, ((), ())), preferred_element_type=jnp.float32)
    return dot(left[0], right_side[0]) + (dot(left[0], right_side[1]) + dot(left[1], right_side[0]))


def block(i):
    return pl.ds(pl.multiple_of(i * 16, 16), 16)


def panel_kernel(where_ref, index_ref, inverse_ref, own_ref, other_ref, near_ref, own_c_ref, other_c_ref, p_ref, both_ref, t_ref, first, second, ordered, factor):
    core, chip = where_ref[0], where_ref[1]
    for k, offset in enumerate((0, -1, 1, 2)):
        at = pl.ds(pl.multiple_of(lax.rem(chip + 4 + offset, 4) * 128, 128), 128)
        own, other = (own_ref[k], other_ref[k]) if k < 3 else (own_c_ref[896:], other_c_ref[896:])
        first[:, at] = jnp.where(core == 0, own, other)
        second[:, at] = jnp.where(core == 0, other, own)
    p_ref[:512, :] = dot3(halves(inverse_ref[0]), halves(first[...]), ((1,), (0,)))
    for i in range(32):
        ordered[16 * i : 16 * i + 16, :] = p_ref[block(index_ref[i]), :]
    blocks = [(near_ref, 0)] + [(own_c_ref, i) for i in range(3)] + [(other_c_ref, i) for i in range(3)]
    for k, (ref, i) in enumerate(blocks):
        for h in range(2):
            for j in range(4):
                source = 256 * i + 128 * h + 32 * j
                factor[64 * k + 32 * h : 64 * k + 32 * h + 32, 128 * j : 128 * j + 128] = ref[source : source + 32, :]
    for j in range(4):
        own, other = (ref[768 + 32 * j : 800 + 32 * j, :] for ref in (own_c_ref, other_c_ref))
        factor[448:480, 128 * j : 128 * j + 128] = jnp.where(core == 1, own, other)
        factor[480:512, 128 * j : 128 * j + 128] = jnp.where(core == 1, other, own)
    coupling = dot3(halves(factor[...]), halves(ordered[...]), ((0,), (0,)))
    p_ref[512:, :] = dot3(halves(inverse_ref[1]), halves(second[...] - coupling), ((1,), (0,)))
    both_ref[:, :512], both_ref[:, 512:] = halves(p_ref[...])
    at = pl.ds(pl.multiple_of(chip * 128, 128), 128)
    for i in range(32):
        t_ref[i] = p_ref[block(2 * i + core), at]


def call(kernel, n_scalars, outs, scratch, *args):
    whole = lambda x: pl.BlockSpec(x.shape, lambda i, *s: (0,) * len(x.shape))
    return pl.pallas_call(
        kernel,
        out_shape=outs,
        grid_spec=pltpu.PrefetchScalarGridSpec(
            num_scalar_prefetch=n_scalars,
            grid=(1,),
            in_specs=[whole(x) for x in args[n_scalars:]],
            out_specs=jax.tree.map(whole, outs),
            scratch_shapes=scratch,
        ),
        compiler_params=pltpu.CompilerParams(vmem_limit_bytes=24 * 2**20),
        cost_estimate=pl.CostEstimate(flops=6 * 512**3, bytes_accessed=4 * 2**20, transcendentals=0),
    )(*args)


def update_kernel(where_ref, a_ref, both_ref, p_ref, l_ref, o_ref):
    row, step = where_ref[2], pl.program_id(0)
    high, low = halves(l_ref[...])
    dims = (((0,), (0,)), ((), ()))
    first = lax.dot_general(high, both_ref[...], dims, preferred_element_type=jnp.float32)
    second = lax.dot_general(low, both_ref[:, :512], dims, preferred_element_type=jnp.float32)
    o_ref[...] = a_ref[...] - (first[:, :512] + (first[:, 512:] + second))

    @pl.when((step == 0) & (row < 2))
    def _():
        o_ref[...] = p_ref[...]


def update(where, a, both, panels, factor):
    depth, columns = panels.shape
    width = 512
    rows = a.shape[0]
    return pl.pallas_call(
        update_kernel,
        out_shape=jax.ShapeDtypeStruct(a.shape, a.dtype),
        grid_spec=pltpu.PrefetchScalarGridSpec(
            num_scalar_prefetch=1,
            grid=(rows // width,),
            in_specs=[
                pl.BlockSpec((width, columns), lambda i, s: (i, 0)),
                pl.BlockSpec(both.shape, lambda i, s: (0, 0)),
                pl.BlockSpec((512, columns), lambda i, s: (jnp.minimum(s[2], 1), 0)),
                pl.BlockSpec((depth, width), lambda i, s: (0, i)),
            ],
            out_specs=pl.BlockSpec((width, columns), lambda i, s: (i, 0)),
        ),
        compiler_params=pltpu.CompilerParams(vmem_limit_bytes=40 * 2**20),
        cost_estimate=pl.CostEstimate(flops=6 * depth * columns * rows, bytes_accessed=20 * 2**20, transcendentals=0),
    )(where, a, both, panels, factor)


def right_kernel(where_ref, inverse_ref, in_ref, l_ref, right_ref, own, y_ref):
    step = pl.program_id(0)

    @pl.when(step == 0)
    def _():
        for j in range(4):
            for c in range(2):
                for t in range(5):
                    own[t, 16 * c : 16 * c + 16, 128 * j : 128 * j + 128] = in_ref[2 * j + c, t]
        y_ref[...] = dot3(halves(own[4]), halves(inverse_ref[0]), ((1,), (1,)))

    y = y_ref[...]
    solved = own[step] - dot3(halves(y), halves(l_ref[...]), ((1,), (0,)))
    solved = jnp.where((step == 0) & (where_ref[2] == 0), y, solved)
    for t in range(4):

        @pl.when(step == t)
        def _():
            right_ref[:, t, :] = solved


def right_panel(where, inverses, pieces, factor):
    return pl.pallas_call(
        right_kernel,
        out_shape=jax.ShapeDtypeStruct((32, 4, 512), factor.dtype),
        grid_spec=pltpu.PrefetchScalarGridSpec(
            num_scalar_prefetch=1,
            grid=(4,),
            in_specs=[
                pl.BlockSpec((1, 512, 512), lambda i, s: (0, 0, 0)),
                pl.BlockSpec(pieces.shape, lambda i, s: (0, 0, 0, 0)),
                pl.BlockSpec((512, 512), lambda i, s: (0, i)),
            ],
            out_specs=pl.BlockSpec((32, 4, 512), lambda i, s: (0, 0, 0)),
            scratch_shapes=[pltpu.VMEM((5, 32, 512), jnp.float32), pltpu.VMEM((32, 512), jnp.float32)],
        ),
        compiler_params=pltpu.CompilerParams(vmem_limit_bytes=24 * 2**20),
        cost_estimate=pl.CostEstimate(flops=6 * 512 * 32 * 2048, bytes_accessed=6 * 2**20, transcendentals=0),
    )(where, inverses, pieces, factor)


def stack(*blocks):
    return jnp.concatenate(blocks, axis=0)


def on_device(a_block, l_panel, inverses):
    row, col = lax.axis_index("row"), lax.axis_index("col")
    core, chip, y, z = row % 2, row // 2, col // Z, col % Z

    where = jnp.stack([core, chip, row]).astype(jnp.int32)

    factor = lax.all_gather(l_panel.reshape(32, 2048), "col", axis=0, tiled=True)

    tile = a_block[0]
    rows = range(ROWS)
    by_chip = lambda *four: jnp.where(chip == 0, four[0], jnp.where(chip == 1, four[1], jnp.where(chip == 2, four[2], four[3])))
    by_y = lambda *four: jnp.where(y == 0, four[0], jnp.where(y == 1, four[1], jnp.where(y == 2, four[2], four[3])))

    piece = stack(*(l_panel[:, 0, 128 * j : 128 * j + 128] for j in range(4)))
    got = lax.ppermute(piece, "row", [(1, 0)])
    quarter = [tile[:, 128 * j : 128 * j + 128] for j in range(4)]
    piece = jnp.where(row == 0, got, piece)
    piece, *quarter = tick(piece, *quarter)

    c2, c1, c3 = (along_x(piece, j, (0, 1)) for j in (2, 1, 3))
    q2, q1, q3 = (along_x(quarter[j], j, (0, 1)) for j in (2, 1, 3))
    piece = by_chip(piece, c1, c2, c3)
    (piece,) = tick(piece)

    near, far, across = along_y(piece, rows, (1, 0)), along_y(piece, rows, (3, 2)), along_y(piece, rows, (2, 3))
    pair = stack(by_y(piece, near, across, far), by_y(near, piece, far, across))
    q = by_chip(quarter[0], q1, q2, q3)
    pair, q = tick(pair, q)

    p1, p4 = from_z(pair, 1), permute(jnp.where(core == 1, pair[:128], pair[128:]), [(flat(r, i, k), flat(r, i, k + 4)) for r in rows for i in range(Y) for k in range(Z)])
    below, above = along_ring_x(q, 1), along_ring_x(q, -1)
    p01 = stack(pair, p1)
    tiles = jnp.stack([q, below, above])
    p01, below, tiles = tick(p01, below, tiles)

    p23 = from_z(p01, 2)
    beyond, other_tiles = along_ring_x(below, 1), swap_cores(tiles)
    rest = stack(p1, p23, p4, beyond)
    rest, other_tiles = tick(rest, other_tiles)
    other_rest = swap_cores(rest)

    c_side = jnp.where(core == 1, 1, -1)
    c_list = (z + c_side * jnp.array((0, 1, 2, 3, -1, -2, -3, 4), jnp.int32)) % Z
    quarters = jnp.arange(4, dtype=jnp.int32)
    c_index = (c_list[:, None] * 2 + (quarters // 2)[None, :] * 16 + (quarters % 2)[None, :]).reshape(-1)
    panels, both, pieces = call(
        panel_kernel,
        2,
        (
            jax.ShapeDtypeStruct((1024, 512), jnp.float32),
            jax.ShapeDtypeStruct((1024, 1024), jnp.bfloat16),
            jax.ShapeDtypeStruct((32, 16, 128), jnp.float32),
        ),
        [pltpu.VMEM((512, 512), jnp.float32)] * 4,
        where, c_index, inverses, tiles, other_tiles, pair, rest, other_rest,
    )

    pieces = lax.all_to_all(pieces, "col", 0, 0, tiled=True).reshape(Y, Z, 16, 128)
    first_tile = jnp.broadcast_to(pieces[0, 0], (ROWS, 1, 16, 128))
    pieces = jnp.concatenate([pieces.transpose(1, 0, 2, 3), first_tile], axis=1)
    pieces = lax.all_to_all(pieces, "row", 0, 0, tiled=True)

    reduced = update(where, a_block.reshape(2048, 512), both, panels, factor)
    pieces, reduced = tick(pieces, reduced)
    right_out = right_panel(where, inverses, pieces, factor)
    return (reduced.reshape(4, 512, 512), right_out)


def solution(mesh):
    return jax.shard_map(
        on_device,
        mesh=mesh,
        in_specs=(P(None, "row", "col"), P("col", None, "row"), P()),
        out_specs=(P(None, "row", "col"), P("col", None, "row")),
        check_vma=False,
    )
```

```python
import jax
import jax.numpy as jnp
from jax import lax
from jax.experimental import pallas as pl
from jax.experimental.pallas import tpu as pltpu
from jax.sharding import PartitionSpec as P

ROWS, Y, Z = 8, 4, 8
COLS = Y * Z


def flat(r, y, z):
    return r * COLS + (y % Y) * Z + z % Z


def permute(x, pairs):
    return lax.ppermute(x, ("row", "col"), pairs)


def tick(*values):
    return lax.optimization_barrier(values)


def along_x(x, j, cores):
    return lax.ppermute(x, "row", [(c, 2 * j + c) for c in cores])


def along_y(x, rows, to):
    return permute(x, [(flat(r, i, k), flat(r, to[i], k)) for r in rows for i in (0, 1) for k in range(Z)])


def swap_cores(x):
    return lax.ppermute(x, "row", [(r, r ^ 1) for r in range(ROWS)])


def from_z(x, distance):
    return permute(x, [
        (flat(r, i, k + (distance if r % 2 else -distance)), flat(r, i, k))
        for r in range(ROWS) for i in range(Y) for k in range(Z)
    ])


def along_ring_x(x, step):
    return lax.ppermute(x, "row", [(r, (r + 2 * step) % ROWS) for r in range(ROWS)])


def halves(x):
    high = x.astype(jnp.bfloat16)
    return high, (x - high.astype(jnp.float32)).astype(jnp.bfloat16)


def dot3(left, right_side, dims):
    dot = lambda u, v: lax.dot_general(u, v, (dims, ((), ())), preferred_element_type=jnp.float32)
    return dot(left[0], right_side[0]) + (dot(left[0], right_side[1]) + dot(left[1], right_side[0]))


def block(i):
    return pl.ds(pl.multiple_of(i * 16, 16), 16)


def panel_kernel(where_ref, index_ref, inverse_ref, own_ref, other_ref, near_ref, own_c_ref, other_c_ref, p_ref, both_ref, t_ref, first, second, ordered, factor):
    core, chip = where_ref[0], where_ref[1]
    for k, offset in enumerate((0, -1, 1, 2)):
        at = pl.ds(pl.multiple_of(lax.rem(chip + 4 + offset, 4) * 128, 128), 128)
        own, other = (own_ref[k], other_ref[k]) if k < 3 else (own_c_ref[896:], other_c_ref[896:])
        first[:, at] = jnp.where(core == 0, own, other)
        second[:, at] = jnp.where(core == 0, other, own)
    p_ref[:512, :] = dot3(halves(inverse_ref[0]), halves(first[...]), ((1,), (0,)))
    for i in range(32):
        ordered[16 * i : 16 * i + 16, :] = p_ref[block(index_ref[i]), :]
    blocks = [(near_ref, 0)] + [(own_c_ref, i) for i in range(3)] + [(other_c_ref, i) for i in range(3)]
    for k, (ref, i) in enumerate(blocks):
        for h in range(2):
            for j in range(4):
                source = 256 * i + 128 * h + 32 * j
                factor[64 * k + 32 * h : 64 * k + 32 * h + 32, 128 * j : 128 * j + 128] = ref[source : source + 32, :]
    for j in range(4):
        own, other = (ref[768 + 32 * j : 800 + 32 * j, :] for ref in (own_c_ref, other_c_ref))
        factor[448:480, 128 * j : 128 * j + 128] = jnp.where(core == 1, own, other)
        factor[480:512, 128 * j : 128 * j + 128] = jnp.where(core == 1, other, own)
    coupling = dot3(halves(factor[...]), halves(ordered[...]), ((0,), (0,)))
    p_ref[512:, :] = dot3(halves(inverse_ref[1]), halves(second[...] - coupling), ((1,), (0,)))
    both_ref[:, :512], both_ref[:, 512:] = halves(p_ref[...])
    at = pl.ds(pl.multiple_of(chip * 128, 128), 128)
    for i in range(32):
        t_ref[i] = p_ref[block(2 * i + core), at]


def call(kernel, n_scalars, outs, scratch, *args):
    whole = lambda x: pl.BlockSpec(x.shape, lambda i, *s: (0,) * len(x.shape))
    return pl.pallas_call(
        kernel,
        out_shape=outs,
        grid_spec=pltpu.PrefetchScalarGridSpec(
            num_scalar_prefetch=n_scalars,
            grid=(1,),
            in_specs=[whole(x) for x in args[n_scalars:]],
            out_specs=jax.tree.map(whole, outs),
            scratch_shapes=scratch,
        ),
        compiler_params=pltpu.CompilerParams(vmem_limit_bytes=24 * 2**20),
        cost_estimate=pl.CostEstimate(flops=6 * 512**3, bytes_accessed=4 * 2**20, transcendentals=0),
    )(*args)


def last_kernel(where_ref, inverse_ref, in_ref, a_ref, both_ref, p_ref, l_ref, o_ref, right_ref, own, y_ref):
    row, step = where_ref[2], pl.program_id(0)

    @pl.when(step == 0)
    def _():
        for j in range(4):
            for c in range(2):
                for t in range(5):
                    own[t, 16 * c : 16 * c + 16, 128 * j : 128 * j + 128] = in_ref[2 * j + c, t]
        y_ref[...] = dot3(halves(own[4]), halves(inverse_ref[0]), ((1,), (1,)))

    high, low = halves(l_ref[...])
    dims = (((0,), (0,)), ((), ()))
    first = lax.dot_general(high, both_ref[...], dims, preferred_element_type=jnp.float32)
    second = lax.dot_general(low, both_ref[:, :512], dims, preferred_element_type=jnp.float32)
    o_ref[...] = a_ref[...] - (first[:, :512] + (first[:, 512:] + second))

    @pl.when((step == 0) & (row < 2))
    def _():
        o_ref[...] = p_ref[...]

    y = y_ref[...]
    solved = own[step] - dot3(halves(y), (high[:512], low[:512]), ((1,), (0,)))
    solved = jnp.where((step == 0) & (row == 0), y, solved)
    for t in range(4):

        @pl.when(step == t)
        def _():
            right_ref[:, t, :] = solved


def last(where, inverses, pieces, a, both, panels, factor):
    depth, columns = panels.shape
    width = 512
    rows = a.shape[0]
    return pl.pallas_call(
        last_kernel,
        out_shape=(jax.ShapeDtypeStruct(a.shape, a.dtype), jax.ShapeDtypeStruct((32, 4, 512), a.dtype)),
        grid_spec=pltpu.PrefetchScalarGridSpec(
            num_scalar_prefetch=1,
            grid=(rows // width,),
            in_specs=[
                pl.BlockSpec((1, 512, 512), lambda i, s: (0, 0, 0)),
                pl.BlockSpec(pieces.shape, lambda i, s: (0, 0, 0, 0)),
                pl.BlockSpec((width, columns), lambda i, s: (i, 0)),
                pl.BlockSpec(both.shape, lambda i, s: (0, 0)),
                pl.BlockSpec((512, columns), lambda i, s: (jnp.minimum(s[2], 1), 0)),
                pl.BlockSpec((depth, width), lambda i, s: (0, i)),
            ],
            out_specs=(
                pl.BlockSpec((width, columns), lambda i, s: (i, 0)),
                pl.BlockSpec((32, 4, 512), lambda i, s: (0, 0, 0)),
            ),
            scratch_shapes=[pltpu.VMEM((5, 32, 512), jnp.float32), pltpu.VMEM((32, 512), jnp.float32)],
        ),
        compiler_params=pltpu.CompilerParams(vmem_limit_bytes=60 * 2**20),
        cost_estimate=pl.CostEstimate(flops=6 * depth * columns * rows, bytes_accessed=20 * 2**20, transcendentals=0),
    )(where, inverses, pieces, a, both, panels, factor)


def stack(*blocks):
    return jnp.concatenate(blocks, axis=0)


def on_device(a_block, l_panel, inverses):
    row, col = lax.axis_index("row"), lax.axis_index("col")
    core, chip, y, z = row % 2, row // 2, col // Z, col % Z

    where = jnp.stack([core, chip, row]).astype(jnp.int32)

    factor = lax.all_gather(l_panel.reshape(32, 2048), "col", axis=0, tiled=True)

    tile = a_block[0]
    rows = range(ROWS)
    by_chip = lambda *four: jnp.where(chip == 0, four[0], jnp.where(chip == 1, four[1], jnp.where(chip == 2, four[2], four[3])))
    by_y = lambda *four: jnp.where(y == 0, four[0], jnp.where(y == 1, four[1], jnp.where(y == 2, four[2], four[3])))

    piece = stack(*(l_panel[:, 0, 128 * j : 128 * j + 128] for j in range(4)))
    got = lax.ppermute(piece, "row", [(1, 0)])
    quarter = [tile[:, 128 * j : 128 * j + 128] for j in range(4)]
    piece = jnp.where(row == 0, got, piece)
    piece, *quarter = tick(piece, *quarter)

    c2, c1, c3 = (along_x(piece, j, (0, 1)) for j in (2, 1, 3))
    q2, q1, q3 = (along_x(quarter[j], j, (0, 1)) for j in (2, 1, 3))
    piece = by_chip(piece, c1, c2, c3)
    (piece,) = tick(piece)

    near, far, across = along_y(piece, rows, (1, 0)), along_y(piece, rows, (3, 2)), along_y(piece, rows, (2, 3))
    pair = stack(by_y(piece, near, across, far), by_y(near, piece, far, across))
    q = by_chip(quarter[0], q1, q2, q3)
    pair, q = tick(pair, q)

    p1, p4 = from_z(pair, 1), permute(jnp.where(core == 1, pair[:128], pair[128:]), [(flat(r, i, k), flat(r, i, k + 4)) for r in rows for i in range(Y) for k in range(Z)])
    below, above = along_ring_x(q, 1), along_ring_x(q, -1)
    p01 = stack(pair, p1)
    tiles = jnp.stack([q, below, above])
    p01, below, tiles = tick(p01, below, tiles)

    p23 = from_z(p01, 2)
    beyond, other_tiles = along_ring_x(below, 1), swap_cores(tiles)
    rest = stack(p1, p23, p4, beyond)
    rest, other_tiles = tick(rest, other_tiles)
    other_rest = swap_cores(rest)

    c_side = jnp.where(core == 1, 1, -1)
    c_list = (z + c_side * jnp.array((0, 1, 2, 3, -1, -2, -3, 4), jnp.int32)) % Z
    quarters = jnp.arange(4, dtype=jnp.int32)
    c_index = (c_list[:, None] * 2 + (quarters // 2)[None, :] * 16 + (quarters % 2)[None, :]).reshape(-1)
    panels, both, pieces = call(
        panel_kernel,
        2,
        (
            jax.ShapeDtypeStruct((1024, 512), jnp.float32),
            jax.ShapeDtypeStruct((1024, 1024), jnp.bfloat16),
            jax.ShapeDtypeStruct((32, 16, 128), jnp.float32),
        ),
        [pltpu.VMEM((512, 512), jnp.float32)] * 4,
        where, c_index, inverses, tiles, other_tiles, pair, rest, other_rest,
    )

    pieces = lax.all_to_all(pieces, "col", 0, 0, tiled=True).reshape(Y, Z, 16, 128)
    first_tile = jnp.broadcast_to(pieces[0, 0], (ROWS, 1, 16, 128))
    pieces = jnp.concatenate([pieces.transpose(1, 0, 2, 3), first_tile], axis=1)
    pieces = lax.all_to_all(pieces, "row", 0, 0, tiled=True)

    reduced, right_out = last(where, inverses, pieces, a_block.reshape(2048, 512), both, panels, factor)
    return (reduced.reshape(4, 512, 512), right_out)


def solution(mesh):
    return jax.shard_map(
        on_device,
        mesh=mesh,
        in_specs=(P(None, "row", "col"), P("col", None, "row"), P()),
        out_specs=(P(None, "row", "col"), P("col", None, "row")),
        check_vma=False,
    )
```

```python
import jax
import jax.numpy as jnp
from jax import lax
from jax.experimental import pallas as pl
from jax.experimental.pallas import tpu as pltpu
from jax.sharding import PartitionSpec as P

ROWS, Y, Z = 8, 4, 8
COLS = Y * Z


def flat(r, y, z):
    return r * COLS + (y % Y) * Z + z % Z


def permute(x, pairs):
    return lax.ppermute(x, ("row", "col"), pairs)


def tick(*values):
    return lax.optimization_barrier(values)


def along_x(x, j, cores):
    return lax.ppermute(x, "row", [(c, 2 * j + c) for c in cores])


def along_y(x, rows, to):
    return permute(x, [(flat(r, i, k), flat(r, to[i], k)) for r in rows for i in (0, 1) for k in range(Z)])


def swap_cores(x):
    return lax.ppermute(x, "row", [(r, r ^ 1) for r in range(ROWS)])


def from_z(x, distance):
    return permute(x, [
        (flat(r, i, k + (distance if r % 2 else -distance)), flat(r, i, k))
        for r in range(ROWS) for i in range(Y) for k in range(Z)
    ])


def along_ring_x(x, step):
    return lax.ppermute(x, "row", [(r, (r + 2 * step) % ROWS) for r in range(ROWS)])


def halves(x):
    high = x.astype(jnp.bfloat16)
    return high, (x - high.astype(jnp.float32)).astype(jnp.bfloat16)


def dot3(left, right_side, dims):
    dot = lambda u, v: lax.dot_general(u, v, (dims, ((), ())), preferred_element_type=jnp.float32)
    return dot(left[0], right_side[0]) + (dot(left[0], right_side[1]) + dot(left[1], right_side[0]))


def block(i):
    return pl.ds(pl.multiple_of(i * 16, 16), 16)


def panel_kernel(where_ref, index_ref, inverse_ref, own_ref, other_ref, near_ref, own_c_ref, other_c_ref, both_ref, t_ref, p_ref, first, second, ordered, factor):
    core, chip = where_ref[0], where_ref[1]
    for k, offset in enumerate((0, -1, 1, 2)):
        at = pl.ds(pl.multiple_of(lax.rem(chip + 4 + offset, 4) * 128, 128), 128)
        own, other = (own_ref[k], other_ref[k]) if k < 3 else (own_c_ref[896:], other_c_ref[896:])
        first[:, at] = jnp.where(core == 0, own, other)
        second[:, at] = jnp.where(core == 0, other, own)
    p_ref[:512, :] = dot3(halves(inverse_ref[0]), halves(first[...]), ((1,), (0,)))
    for i in range(32):
        ordered[16 * i : 16 * i + 16, :] = p_ref[block(index_ref[i]), :]
    blocks = [(near_ref, 0)] + [(own_c_ref, i) for i in range(3)] + [(other_c_ref, i) for i in range(3)]
    for k, (ref, i) in enumerate(blocks):
        for h in range(2):
            for j in range(4):
                source = 256 * i + 128 * h + 32 * j
                factor[64 * k + 32 * h : 64 * k + 32 * h + 32, 128 * j : 128 * j + 128] = ref[source : source + 32, :]
    for j in range(4):
        own, other = (ref[768 + 32 * j : 800 + 32 * j, :] for ref in (own_c_ref, other_c_ref))
        factor[448:480, 128 * j : 128 * j + 128] = jnp.where(core == 1, own, other)
        factor[480:512, 128 * j : 128 * j + 128] = jnp.where(core == 1, other, own)
    coupling = dot3(halves(factor[...]), halves(ordered[...]), ((0,), (0,)))
    p_ref[512:, :] = dot3(halves(inverse_ref[1]), halves(second[...] - coupling), ((1,), (0,)))
    both_ref[:, :512], both_ref[:, 512:] = halves(p_ref[...])
    at = pl.ds(pl.multiple_of(chip * 128, 128), 128)
    for i in range(32):
        t_ref[i] = p_ref[block(2 * i + core), at]


def call(kernel, n_scalars, outs, scratch, *args):
    whole = lambda x: pl.BlockSpec(x.shape, lambda i, *s: (0,) * len(x.shape))
    return pl.pallas_call(
        kernel,
        out_shape=outs,
        grid_spec=pltpu.PrefetchScalarGridSpec(
            num_scalar_prefetch=n_scalars,
            grid=(1,),
            in_specs=[whole(x) for x in args[n_scalars:]],
            out_specs=jax.tree.map(whole, outs),
            scratch_shapes=scratch,
        ),
        compiler_params=pltpu.CompilerParams(vmem_limit_bytes=24 * 2**20),
        cost_estimate=pl.CostEstimate(flops=6 * 512**3, bytes_accessed=4 * 2**20, transcendentals=0),
    )(*args)


def last_kernel(where_ref, inverse_ref, in_ref, a_ref, both_ref, l_ref, o_ref, right_ref, own, y_ref):
    row, step = where_ref[2], pl.program_id(0)

    @pl.when(step == 0)
    def _():
        for j in range(4):
            for c in range(2):
                for t in range(5):
                    own[t, 16 * c : 16 * c + 16, 128 * j : 128 * j + 128] = in_ref[2 * j + c, t]
        y_ref[...] = dot3(halves(own[4]), halves(inverse_ref[0]), ((1,), (1,)))

    high, low = halves(l_ref[...])
    dims = (((0,), (0,)), ((), ()))
    first = lax.dot_general(high, both_ref[...], dims, preferred_element_type=jnp.float32)
    second = lax.dot_general(low, both_ref[:, :512], dims, preferred_element_type=jnp.float32)
    o_ref[...] = a_ref[...] - (first[:, :512] + (first[:, 512:] + second))

    @pl.when((step == 0) & (row < 2))
    def _():
        at = pl.ds(pl.multiple_of(jnp.minimum(row, 1) * 512, 512), 512)
        o_ref[...] = both_ref[at, :512].astype(jnp.float32) + both_ref[at, 512:].astype(jnp.float32)

    y = y_ref[...]
    solved = own[step] - dot3(halves(y), (high[:512], low[:512]), ((1,), (0,)))
    solved = jnp.where((step == 0) & (row == 0), y, solved)
    for t in range(4):

        @pl.when(step == t)
        def _():
            right_ref[:, t, :] = solved


def last(where, inverses, pieces, a, both, factor):
    depth, columns = both.shape[0], both.shape[1] // 2
    width = 512
    rows = a.shape[0]
    return pl.pallas_call(
        last_kernel,
        out_shape=(jax.ShapeDtypeStruct(a.shape, a.dtype), jax.ShapeDtypeStruct((32, 4, 512), a.dtype)),
        grid_spec=pltpu.PrefetchScalarGridSpec(
            num_scalar_prefetch=1,
            grid=(rows // width,),
            in_specs=[
                pl.BlockSpec((1, 512, 512), lambda i, s: (0, 0, 0)),
                pl.BlockSpec(pieces.shape, lambda i, s: (0, 0, 0, 0)),
                pl.BlockSpec((width, columns), lambda i, s: (i, 0)),
                pl.BlockSpec(both.shape, lambda i, s: (0, 0)),
                pl.BlockSpec((depth, width), lambda i, s: (0, i)),
            ],
            out_specs=(
                pl.BlockSpec((width, columns), lambda i, s: (i, 0)),
                pl.BlockSpec((32, 4, 512), lambda i, s: (0, 0, 0)),
            ),
            scratch_shapes=[pltpu.VMEM((5, 32, 512), jnp.float32), pltpu.VMEM((32, 512), jnp.float32)],
        ),
        compiler_params=pltpu.CompilerParams(vmem_limit_bytes=60 * 2**20),
        cost_estimate=pl.CostEstimate(flops=6 * depth * columns * rows, bytes_accessed=20 * 2**20, transcendentals=0),
    )(where, inverses, pieces, a, both, factor)


def stack(*blocks):
    return jnp.concatenate(blocks, axis=0)


def on_device(a_block, l_panel, inverses):
    row, col = lax.axis_index("row"), lax.axis_index("col")
    core, chip, y, z = row % 2, row // 2, col // Z, col % Z

    where = jnp.stack([core, chip, row]).astype(jnp.int32)

    factor = lax.all_gather(l_panel.reshape(32, 2048), "col", axis=0, tiled=True)

    tile = a_block[0]
    rows = range(ROWS)
    by_chip = lambda *four: jnp.where(chip == 0, four[0], jnp.where(chip == 1, four[1], jnp.where(chip == 2, four[2], four[3])))
    by_y = lambda *four: jnp.where(y == 0, four[0], jnp.where(y == 1, four[1], jnp.where(y == 2, four[2], four[3])))

    piece = stack(*(l_panel[:, 0, 128 * j : 128 * j + 128] for j in range(4)))
    got = lax.ppermute(piece, "row", [(1, 0)])
    quarter = [tile[:, 128 * j : 128 * j + 128] for j in range(4)]
    piece = jnp.where(row == 0, got, piece)
    piece, *quarter = tick(piece, *quarter)

    c2, c1, c3 = (along_x(piece, j, (0, 1)) for j in (2, 1, 3))
    q2, q1, q3 = (along_x(quarter[j], j, (0, 1)) for j in (2, 1, 3))
    piece = by_chip(piece, c1, c2, c3)
    (piece,) = tick(piece)

    near, far, across = along_y(piece, rows, (1, 0)), along_y(piece, rows, (3, 2)), along_y(piece, rows, (2, 3))
    pair = stack(by_y(piece, near, across, far), by_y(near, piece, far, across))
    q = by_chip(quarter[0], q1, q2, q3)
    pair, q = tick(pair, q)

    p1, p4 = from_z(pair, 1), permute(jnp.where(core == 1, pair[:128], pair[128:]), [(flat(r, i, k), flat(r, i, k + 4)) for r in rows for i in range(Y) for k in range(Z)])
    below, above = along_ring_x(q, 1), along_ring_x(q, -1)
    p01 = stack(pair, p1)
    tiles = jnp.stack([q, below, above])
    p01, below, tiles = tick(p01, below, tiles)

    p23 = from_z(p01, 2)
    beyond, other_tiles = along_ring_x(below, 1), swap_cores(tiles)
    rest = stack(p1, p23, p4, beyond)
    rest, other_tiles = tick(rest, other_tiles)
    other_rest = swap_cores(rest)

    c_side = jnp.where(core == 1, 1, -1)
    c_list = (z + c_side * jnp.array((0, 1, 2, 3, -1, -2, -3, 4), jnp.int32)) % Z
    quarters = jnp.arange(4, dtype=jnp.int32)
    c_index = (c_list[:, None] * 2 + (quarters // 2)[None, :] * 16 + (quarters % 2)[None, :]).reshape(-1)
    both, pieces = call(
        panel_kernel,
        2,
        (
            jax.ShapeDtypeStruct((1024, 1024), jnp.bfloat16),
            jax.ShapeDtypeStruct((32, 16, 128), jnp.float32),
        ),
        [pltpu.VMEM((1024, 512), jnp.float32)] + [pltpu.VMEM((512, 512), jnp.float32)] * 4,
        where, c_index, inverses, tiles, other_tiles, pair, rest, other_rest,
    )

    pieces = lax.all_to_all(pieces, "col", 0, 0, tiled=True).reshape(Y, Z, 16, 128)
    first_tile = jnp.broadcast_to(pieces[0, 0], (ROWS, 1, 16, 128))
    pieces = jnp.concatenate([pieces.transpose(1, 0, 2, 3), first_tile], axis=1)
    pieces = lax.all_to_all(pieces, "row", 0, 0, tiled=True)

    reduced, right_out = last(where, inverses, pieces, a_block.reshape(2048, 512), both, factor)
    return (reduced.reshape(4, 512, 512), right_out)


def solution(mesh):
    return jax.shard_map(
        on_device,
        mesh=mesh,
        in_specs=(P(None, "row", "col"), P("col", None, "row"), P()),
        out_specs=(P(None, "row", "col"), P("col", None, "row")),
        check_vma=False,
    )
```
